32 devices in a mesh: groups: 2 (over y), row: 4 (over z), col: 4 (over x, core).
Axes of the slice: x: 2, y: 2, z: 4, core: 2. Of those that a mesh axis runs over, the one named last changes fastest.
Arguments:
- tokens: bfloat16 [1024, 4096], P(('groups', 'row'), 'col'), parts along dimension 0, may hold values from -90 to 90
- norm_gain: float32 [4096], P('col'), may hold values from 0.5 to 1.5
- gate_weight: bfloat16 [4096, 16384], P('col', 'row'), may hold values from -0.09375 to 0.09375
- up_weight: bfloat16 [4096, 16384], P('col', 'row'), may hold values from -0.09375 to 0.09375
- down_weight: bfloat16 [16384, 4096], P('row', 'col'), may hold values from -0.046875 to 0.046875
Outputs:
- block_out: bfloat16 [1024, 4096], P(('groups', 'row'), 'col'), parts along dimension 0
The draws below stay inside these ranges and needn't reach their ends.
There are 2 independent parts, one for each index of `groups`. The reference program is written for one: setup_inputs(seed, part) draws one part's arguments, and reference() takes and returns one part's arrays. A program takes and returns all parts, laid end to end along the dimension named above; an argument that names none is the same for every part. Nothing has to cross between parts.
All inputs are finite; a program needn't handle non-finite values.
Results may differ from the reference program's by a relative error of at most 0.02.
Values may be sent and summed in bfloat16 or wider, within the bound.
A program may use at most 128 MiB of HBM per device.

```python
import math
import jax
import jax.numpy as jnp
from jax import lax

D = 4096
FF = 16384
TOKENS = 512
N_ROW = 4
N_COL = 4


def draw_tokens(key, part):
    first_key, second_key, third_key = jax.random.split(jax.random.fold_in(key, 17), 3)
    columns = jnp.arange(D, dtype=jnp.float32) / D
    rising = jnp.exp(0.5 * math.log(3.0) * columns)
    column_factor = jnp.exp(jax.random.uniform(second_key, (D,), jnp.float32, 0.0, math.log(3.2)))
    row_factor = jnp.exp(jax.random.uniform(third_key, (TOKENS, 1), jnp.float32, math.log(0.3), math.log(3.0)))
    base = jnp.clip(jax.random.normal(first_key, (TOKENS, D), jnp.float32), -5.0, 5.0)
    return (base * row_factor * column_factor[None, :] * rising[None, :]).astype(jnp.bfloat16)


def shard_levels(own_key, extent, cuts, smallest, top_value):
    level = 1.0
    for axis_at, shards_of in cuts:
        steps = jax.random.uniform(jax.random.fold_in(jax.random.fold_in(own_key, 6), axis_at), (shards_of,), jnp.float32, smallest / len(cuts), top_value / len(cuts))
        level = level * jnp.repeat(jnp.exp(steps), extent[axis_at] // shards_of).reshape((-1,) + (1,) * (len(extent) - 1 - axis_at))
    return level


def gaussian(rng, extent, scale, reach, shards=(), kind=jnp.bfloat16):
    loudness = shard_levels(rng, extent, shards, -0.22, 0.18) if shards else 1.0
    values = jax.random.normal(rng, extent, jnp.float32) * scale * loudness
    return jnp.minimum(jnp.maximum(values, -reach), reach).astype(kind)


def setup_inputs(seed: int = 0, part: int = 0) -> dict:
    key_of = jax.random.split(jax.random.key(seed), 6)
    own_keys = jax.random.split(jax.random.fold_in(key_of[5], part), 6)
    return {
        "tokens": draw_tokens(jax.random.fold_in(jax.random.fold_in(key_of[5], part), 71), part),
        "norm_gain": jnp.clip(0.5 + 1.0 * jax.random.uniform(key_of[1], (D,), jnp.float32) ** shard_levels(key_of[1], (D,), ((0, 4),), -0.2, 0.2), 0.5, 1.5),
        "gate_weight": gaussian(key_of[2], (D, FF), D ** -0.5, 0.09375, ((0, 4), (1, 4))),
        "up_weight": gaussian(key_of[3], (D, FF), D ** -0.5, 0.09375, ((0, 4), (1, 4))),
        "down_weight": gaussian(key_of[4], (FF, D), FF ** -0.5, 0.046875, ((0, 4), (1, 4))),
    }


epsilon = 1e-05

def blocked(left, right, parts):
    width = left.shape[1] // parts
    total = jnp.zeros((left.shape[0], right.shape[1]), jnp.float32)
    for index in range(parts):
        product = jnp.dot(left[:, index * width:(index + 1) * width], right[index * width:(index + 1) * width, :], preferred_element_type=jnp.float32)
        rounded = lax.optimization_barrier(product.astype(jnp.bfloat16))
        total = total + rounded.astype(jnp.float32)
    return total

def reference(tokens, norm_gain, gate_weight, up_weight, down_weight):
    widened = tokens.astype(jnp.float32)
    inverse_rms = lax.rsqrt(lax.optimization_barrier(jnp.mean(widened * widened, axis=1, keepdims=True)) + epsilon)
    normed = (widened * inverse_rms * norm_gain[None, :]).astype(jnp.bfloat16)
    gate = blocked(normed, gate_weight, N_COL)
    up_sum = blocked(normed, up_weight, N_COL)
    hidden = (jax.nn.silu(gate) * up_sum).astype(jnp.bfloat16)
    return blocked(hidden, down_weight, N_ROW).astype(jnp.bfloat16)
```

```python
import functools
import jax
import jax.numpy as jnp
from jax import lax
from jax.experimental import pallas as pl
from jax.experimental.pallas import tpu as pltpu
from jax.sharding import PartitionSpec as P

epsilon = 1e-05
MESH = pl.DeviceIdType.MESH
f32 = jnp.float32
bf16 = jnp.bfloat16


def remote(src, dst, send, recv, device):
    return pltpu.make_async_remote_copy(
        src_ref=src, dst_ref=dst, send_sem=send, recv_sem=recv, device_id=device, device_id_type=MESH
    )


def kernel(n, width_total, tok, gain, gate_w, up_w, down_w, out,
           w_v, wd_v, xg, a_s, a_r, b_s, b_r, p_own, p_b, hid, q_s, q_r, o_s, o_r,
           w_sem, own_sem, t_ss, t_rs, a_ss, a_rs, b_ss, b_rs, h_ss, h_rs, q_ss, q_rs, o_ss, o_rs):
    T, width = tok.shape
    F = gate_w.shape[1] // 4
    tile_f = min(256, F)
    tile_d = min(256, width)
    row = lax.axis_index("row")
    col = lax.axis_index("col")
    hi, lo = col // 2, col % 2
    sibling = hi * 2 + (1 - lo)
    across = (1 - hi) * 2 + lo
    diagonal = (1 - hi) * 2 + (1 - lo)
    shards = (diagonal, across, sibling, col)

    def row_at(step):
        return lax.rem(row + step, n)

    def row_back(step):
        return lax.rem(row + n - step, n)

    def load(role, g):
        at = pl.ds(pl.multiple_of(shards[role] * F, F), F)
        source = (gate_w, up_w)[g].at[:, at]
        return pltpu.make_async_copy(source, w_v.at[role, g], w_sem.at[g, role])

    def load_down(role):
        at = pl.ds(pl.multiple_of(shards[role] * F, F), F)
        return pltpu.make_async_copy(down_w.at[at, :], wd_v.at[role], w_sem.at[2, role])

    def send_tokens(i):
        return remote(tok, xg.at[i], t_ss.at[i], t_rs.at[i], {"row": row_back(i)})

    def send_half(i, which):
        return remote(a_s.at[i, which], a_r.at[i, which], a_ss.at[i, which], a_rs.at[i, which], {"col": sibling})

    def send_chip(i):
        return remote(b_s.at[i], b_r.at[i], b_ss.at[i], b_rs.at[i], {"col": across})

    def send_hidden(i, which):
        source, target, device = ((3, 1, across), (3, 2, sibling), (1, 0, sibling))[which]
        return remote(hid.at[i, source], hid.at[i, target], h_ss.at[i, which], h_rs.at[i, which], {"col": device})

    def send_squares(i, role):
        return remote(q_s.at[i], q_r.at[i, role], q_ss.at[i, role], q_rs.at[i, role], {"col": shards[role]})

    def send_out(i):
        return remote(o_s.at[i], o_r.at[i], o_ss.at[i], o_rs.at[i], {"row": row_at(i)})

    own_tokens = pltpu.make_async_copy(tok, xg.at[0], own_sem)
    own_tokens.start()
    for role in range(4):
        for g in range(2):
            load(role, g).start()

    barrier = pltpu.get_barrier_semaphore()

    @pl.loop(1, n)
    def _(i):
        pl.semaphore_signal(barrier, inc=1, device_id={"row": row_at(i)}, device_id_type=MESH)

    for peer in shards[:3]:
        pl.semaphore_signal(barrier, inc=1, device_id={"col": peer}, device_id_type=MESH)
    pl.semaphore_wait(barrier, n + 2)

    @pl.loop(1, n)
    def _(i):
        send_tokens(i).start()

    for role in range(4):
        load_down(role).start()

    def project(i, role, store):
        @pl.when(i == 0)
        def _():
            for g in range(2):
                load(role, g).wait()

        x = xg[i]
        for g in range(2):
            @pl.loop(0, F // tile_f)
            def _(t):
                at = pl.ds(pl.multiple_of(t * tile_f, tile_f), tile_f)
                store(g, at, jnp.dot(x, w_v[role, g, :, at], preferred_element_type=f32))

    def partials(i):
        @pl.when(i == 0)
        def _():
            own_tokens.wait()

        @pl.when(i > 0)
        def _():
            send_tokens(i).wait_recv()

        x = xg[i].astype(f32)
        squares = x * x
        lanes = squares[:, :128]
        for c in range(1, width // 128):
            lanes = lanes + squares[:, c * 128:(c + 1) * 128]
        total = jnp.sum(lanes.T, axis=0, keepdims=True)
        q_s[i] = jnp.broadcast_to(total, (8, T))
        xg[i] = (x * gain[...]).astype(bf16)
        for role in range(3):
            send_squares(i, role).start()

        def to_half(which):
            def store(g, at, value):
                a_s[i, which, g, :, at] = value.astype(bf16)
            return store

        def to_chip(g, at, value):
            p_b[g, :, at] = value

        def to_own(g, at, value):
            p_own[lax.rem(i, 2), g, :, at] = value

        project(i, 0, to_half(0))
        send_half(i, 0).start()
        project(i, 1, to_chip)
        send_half(i, 0).wait_recv()
        for g in range(2):
            @pl.loop(0, F // tile_f)
            def _(t):
                at = pl.ds(pl.multiple_of(t * tile_f, tile_f), tile_f)
                b_s[i, g, :, at] = (p_b[g, :, at] + a_r[i, 0, g, :, at].astype(f32)).astype(bf16)
        send_chip(i).start()
        project(i, 2, to_half(1))
        send_half(i, 1).start()
        project(i, 3, to_own)

    def activate(i):
        for role in range(3):
            send_squares(i, role).wait_recv()
        send_half(i, 1).wait_recv()
        send_chip(i).wait_recv()
        total = q_s[i] + q_r[i, 0] + q_r[i, 1] + q_r[i, 2]
        inverse = lax.rsqrt(total / width_total + epsilon)
        inverse = jnp.broadcast_to(inverse[0:1, :], (128, T)).T[:, 0:1]
        slot = lax.rem(i, 2)

        @pl.loop(0, F // tile_f)
        def _(t):
            at = pl.ds(pl.multiple_of(t * tile_f, tile_f), tile_f)
            gate, up = (
                (p_own[slot, g, :, at] + a_r[i, 1, g, :, at].astype(f32) + b_r[i, g, :, at].astype(f32)) * inverse
                for g in range(2)
            )
            hid[i, 3, :, at] = (gate / (1.0 + jnp.exp(-gate)) * up).astype(bf16)

        send_hidden(i, 0).start()
        send_hidden(i, 1).start()

    def lower(i):
        @pl.when(i == 0)
        def _():
            for role in range(4):
                load_down(role).wait()

        send_hidden(i, 0).wait_recv()
        send_hidden(i, 2).start()
        send_hidden(i, 1).wait_recv()
        send_hidden(i, 2).wait_recv()

        @pl.loop(0, width // tile_d)
        def _(t):
            at = pl.ds(pl.multiple_of(t * tile_d, tile_d), tile_d)
            total = jnp.dot(hid[i, 3], wd_v[3, :, at], preferred_element_type=f32)
            for role in range(3):
                total += jnp.dot(hid[i, role], wd_v[role, :, at], preferred_element_type=f32)
            o_s[i, :, at] = total.astype(bf16)

        @pl.when(i > 0)
        def _():
            send_out(i).start()

    @pl.loop(0, n + 2)
    def _(step):
        @pl.when(step < n)
        def _():
            partials(step)

        @pl.when((step >= 1) & (step < n + 1))
        def _():
            activate(step - 1)

        @pl.when(step >= 2)
        def _():
            lower(step - 2)

    @pl.loop(1, n)
    def _(i):
        send_out(i).wait_recv()

    @pl.loop(0, width // tile_d)
    def _(t):
        at = pl.ds(pl.multiple_of(t * tile_d, tile_d), tile_d)
        out[:, at] = lax.fori_loop(
            1, n, lambda i, total: total + o_r[i, :, at].astype(f32), o_s[0, :, at].astype(f32)
        ).astype(bf16)

    @pl.loop(0, n)
    def _(i):
        @pl.when(i > 0)
        def _():
            send_tokens(i).wait_send()
            send_out(i).wait_send()

        send_half(i, 0).wait_send()
        send_half(i, 1).wait_send()
        send_chip(i).wait_send()
        for which in range(3):
            send_hidden(i, which).wait_send()
            send_squares(i, which).wait_send()


def per_device(n, tokens, norm_gain, gate_weight, up_weight, down_weight):
    T, width = tokens.shape
    F = gate_weight.shape[1] // 4
    dma = pltpu.SemaphoreType.DMA
    anywhere = pl.BlockSpec(memory_space=pl.ANY)
    vmem = pl.BlockSpec(memory_space=pltpu.VMEM)
    return pl.pallas_call(
        functools.partial(kernel, n, width * 4),
        out_shape=jax.ShapeDtypeStruct((T, width), bf16),
        in_specs=[anywhere, vmem, anywhere, anywhere, anywhere],
        out_specs=vmem,
        scratch_shapes=[
            pltpu.VMEM((4, 2, width, F), bf16),
            pltpu.VMEM((4, F, width), bf16),
            pltpu.VMEM((n, T, width), bf16),
            pltpu.VMEM((n, 2, 2, T, F), bf16),
            pltpu.VMEM((n, 2, 2, T, F), bf16),
            pltpu.VMEM((n, 2, T, F), bf16),
            pltpu.VMEM((n, 2, T, F), bf16),
            pltpu.VMEM((2, 2, T, F), f32),
            pltpu.VMEM((2, T, F), f32),
            pltpu.VMEM((n, 4, T, F), bf16),
            pltpu.VMEM((n, 8, T), f32),
            pltpu.VMEM((n, 3, 8, T), f32),
            pltpu.VMEM((n, T, width), bf16),
            pltpu.VMEM((n, T, width), bf16),
            dma((3, 4)), dma(()),
            dma((n,)), dma((n,)),
            dma((n, 2)), dma((n, 2)),
            dma((n,)), dma((n,)),
            dma((n, 3)), dma((n, 3)),
            dma((n, 3)), dma((n, 3)),
            dma((n,)), dma((n,)),
        ],
        compiler_params=pltpu.CompilerParams(
            collective_id=0, has_side_effects=True, vmem_limit_bytes=58 * 1024 * 1024
        ),
    )(tokens, norm_gain[None, :], gate_weight, up_weight, down_weight)


def solution(mesh):
    placed = (
        P(("groups", "row"), "col"),
        P("col"),
        P("col", "row"),
        P("col", "row"),
        P("row", "col"),
    )
    return jax.shard_map(
        functools.partial(per_device, mesh.shape["row"]),
        mesh=mesh,
        in_specs=placed,
        out_specs=P(("groups", "row"), "col"),
        check_vma=False,
    )
```

```python
import functools
import jax
import jax.numpy as jnp
from jax import lax
from jax.experimental import pallas as pl
from jax.experimental.pallas import tpu as pltpu
from jax.sharding import PartitionSpec as P

epsilon = 1e-05
MESH = pl.DeviceIdType.MESH
f32 = jnp.float32
bf16 = jnp.bfloat16


def remote(src, dst, send, recv, device):
    return pltpu.make_async_remote_copy(
        src_ref=src, dst_ref=dst, send_sem=send, recv_sem=recv, device_id=device, device_id_type=MESH
    )


def kernel(n, width_total, tok, gain, gate_w, up_w, down_w, out,
           w_v, wd_v, xg, a_s, a_r, b_s, b_r, p_own, p_b, hid, q_s, q_r, o_s, o_r, total,
           w_sem, own_sem, t_ss, t_rs, a_ss, a_rs, b_ss, b_rs, h_ss, h_rs, q_ss, q_rs, o_ss, o_rs):
    T, width = tok.shape
    rows = T // 2
    F = gate_w.shape[1] // 4
    tile_f = min(256, F)
    tile_d = min(256, width)
    row = lax.axis_index("row")
    col = lax.axis_index("col")
    hi, lo = col // 2, col % 2
    sibling = hi * 2 + (1 - lo)
    across = (1 - hi) * 2 + lo
    diagonal = (1 - hi) * 2 + (1 - lo)
    shards = (diagonal, across, sibling, col)

    def shift(step):
        late = jnp.where(step == n - 1, n - 1, jnp.where(step == n - 2, 1, step + 1))
        return jnp.where(step == 0, 0, late)

    def row_at(step):
        return lax.rem(row + shift(step), n)

    def row_back(step):
        return lax.rem(row + n - shift(step), n)

    def load(role, g):
        at = pl.ds(pl.multiple_of(shards[role] * F, F), F)
        source = (gate_w, up_w)[g].at[:, at]
        return pltpu.make_async_copy(source, w_v.at[role, g], w_sem.at[g, role])

    def load_down(role):
        at = pl.ds(pl.multiple_of(shards[role] * F, F), F)
        return pltpu.make_async_copy(down_w.at[at, :], wd_v.at[role], w_sem.at[2, role])

    def send_tokens(i):
        return remote(tok, xg.at[i], t_ss.at[i], t_rs.at[i], {"row": row_back(i)})

    def send_half(i, which, g):
        return remote(a_s.at[i, which, g], a_r.at[i, which, g],
                      a_ss.at[i, which, g], a_rs.at[i, which, g], {"col": sibling})

    def send_chip(i, g):
        return remote(b_s.at[i, g], b_r.at[i, g], b_ss.at[i, g], b_rs.at[i, g], {"col": across})

    def send_hidden(i, which, half):
        source, target, device = ((3, 1, across), (3, 2, sibling), (1, 0, sibling))[which]
        at = pl.ds(half * rows, rows)
        return remote(hid.at[i, source, at], hid.at[i, target, at],
                      h_ss.at[i, which, half], h_rs.at[i, which, half], {"col": device})

    def send_squares(i, role):
        return remote(q_s.at[i], q_r.at[i, role], q_ss.at[i, role], q_rs.at[i, role], {"col": shards[role]})

    def send_out(i, half):
        return remote(o_s.at[i, half], o_r.at[i, half], o_ss.at[i, half], o_rs.at[i, half], {"row": row_at(i)})

    own_tokens = pltpu.make_async_copy(tok, xg.at[0], own_sem)
    own_tokens.start()
    for g in range(2):
        for role in range(2):
            load(role, g).start()

    barrier = pltpu.get_barrier_semaphore()

    @pl.loop(1, n)
    def _(i):
        pl.semaphore_signal(barrier, inc=1, device_id={"row": row_at(i)}, device_id_type=MESH)

    for peer in shards[:3]:
        pl.semaphore_signal(barrier, inc=1, device_id={"col": peer}, device_id_type=MESH)
    pl.semaphore_wait(barrier, n + 2)

    if n > 1:
        send_tokens(1).start()

    for role in range(2, 4):
        for g in range(2):
            load(role, g).start()
    for role in range(4):
        load_down(role).start()

    def project(i, role, g, store):
        @pl.when(i == 0)
        def _():
            load(role, g).wait()

        x = xg[i]

        @pl.loop(0, F // tile_f)
        def _(t):
            at = pl.ds(pl.multiple_of(t * tile_f, tile_f), tile_f)
            store(g, at, jnp.dot(x, w_v[role, g, :, at], preferred_element_type=f32))

    def partials(i):
        @pl.when(i == 0)
        def _():
            own_tokens.wait()

        @pl.when(i > 0)
        def _():
            send_tokens(i).wait_recv()

        @pl.when((i > 0) & (i + 1 < n))
        def _():
            send_tokens(i + 1).start()

        x = xg[i].astype(f32)
        squares = x * x
        lanes = squares[:, :128]
        for c in range(1, width // 128):
            lanes = lanes + squares[:, c * 128:(c + 1) * 128]
        q_s[i] = jnp.broadcast_to(jnp.sum(lanes.T, axis=0, keepdims=True), (8, T))
        xg[i] = (x * gain[...]).astype(bf16)
        for role in range(3):
            send_squares(i, role).start()

        def to_half(which):
            def store(g, at, value):
                a_s[i, which, g, :, at] = value.astype(bf16)
            return store

        def to_chip(g, at, value):
            p_b[g, :, at] = value

        def to_own(g, at, value):
            p_own[lax.rem(i, 2), g, :, at] = value

        for g in range(2):
            project(i, 0, g, to_half(0))
            send_half(i, 0, g).start()
            project(i, 1, g, to_chip)
            send_half(i, 0, g).wait_recv()

            @pl.loop(0, F // tile_f)
            def _(t):
                at = pl.ds(pl.multiple_of(t * tile_f, tile_f), tile_f)
                b_s[i, g, :, at] = (p_b[g, :, at] + a_r[i, 0, g, :, at].astype(f32)).astype(bf16)

            send_chip(i, g).start()

        for g in range(2):
            project(i, 2, g, to_half(1))
            send_half(i, 1, g).start()
        for g in range(2):
            project(i, 3, g, to_own)

    def activate(i):
        for role in range(3):
            send_squares(i, role).wait_recv()
        for g in range(2):
            send_half(i, 1, g).wait_recv()
            send_chip(i, g).wait_recv()
        all_squares = q_s[i] + q_r[i, 0] + q_r[i, 1] + q_r[i, 2]
        inverse = lax.rsqrt(all_squares / width_total + epsilon)
        inverse = jnp.broadcast_to(inverse[0:1, :], (128, T)).T[:, 0:1]
        slot = lax.rem(i, 2)

        for half in range(2):
            part = pl.ds(half * rows, rows)
            factor = inverse[half * rows:(half + 1) * rows]

            @pl.loop(0, F // tile_f)
            def _(t):
                at = pl.ds(pl.multiple_of(t * tile_f, tile_f), tile_f)
                gate, up = (
                    (p_own[slot, g, part, at] + a_r[i, 1, g, part, at].astype(f32)
                     + b_r[i, g, part, at].astype(f32)) * factor
                    for g in range(2)
                )
                hid[i, 3, part, at] = (gate / (1.0 + jnp.exp(-gate)) * up).astype(bf16)

            send_hidden(i, 0, half).start()
            send_hidden(i, 1, half).start()

    def lower(i):
        @pl.when(i == 0)
        def _():
            for role in range(4):
                load_down(role).wait()

        for half in range(2):
            send_hidden(i, 1, half).wait_recv()

        def product(role, part, at):
            return jnp.dot(hid[i, role, part], wd_v[role, :, at], preferred_element_type=f32)

        @pl.loop(0, width // tile_d)
        def _(t):
            at = pl.ds(pl.multiple_of(t * tile_d, tile_d), tile_d)
            every = pl.ds(0, T)
            total[:, at] = product(3, every, at) + product(2, every, at)

        for half in range(2):
            part = pl.ds(half * rows, rows)
            send_hidden(i, 0, half).wait_recv()
            send_hidden(i, 2, half).start()

            @pl.loop(0, width // tile_d)
            def _(t):
                at = pl.ds(pl.multiple_of(t * tile_d, tile_d), tile_d)
                total[part, at] += product(1, part, at)

            send_hidden(i, 2, half).wait_recv()

            @pl.loop(0, width // tile_d)
            def _(t):
                at = pl.ds(pl.multiple_of(t * tile_d, tile_d), tile_d)
                o_s[i, half, :, at] = (total[part, at] + product(0, part, at)).astype(bf16)

            @pl.when(i > 0)
            def _():
                send_out(i, half).start()

    @pl.loop(0, n + 2)
    def _(step):
        @pl.when(step < n)
        def _():
            partials(step)

        @pl.when((step >= 1) & (step < n + 1))
        def _():
            activate(step - 1)

        @pl.when(step >= 2)
        def _():
            lower(step - 2)

    for half in range(2):
        @pl.loop(1, n)
        def _(i):
            send_out(i, half).wait_recv()

        @pl.loop(0, width // tile_d)
        def _(t):
            at = pl.ds(pl.multiple_of(t * tile_d, tile_d), tile_d)
            out[pl.ds(half * rows, rows), at] = lax.fori_loop(
                1, n, lambda i, so_far: so_far + o_r[i, half, :, at].astype(f32), o_s[0, half, :, at].astype(f32)
            ).astype(bf16)

    @pl.loop(0, n)
    def _(i):
        @pl.when(i > 0)
        def _():
            send_tokens(i).wait_send()
            send_out(i, 0).wait_send()
            send_out(i, 1).wait_send()

        for piece in range(2):
            send_half(i, 0, piece).wait_send()
            send_half(i, 1, piece).wait_send()
            send_chip(i, piece).wait_send()
        for which in range(3):
            for half in range(2):
                send_hidden(i, which, half).wait_send()
            send_squares(i, which).wait_send()


def per_device(n, tokens, norm_gain, gate_weight, up_weight, down_weight):
    T, width = tokens.shape
    F = gate_weight.shape[1] // 4
    dma = pltpu.SemaphoreType.DMA
    anywhere = pl.BlockSpec(memory_space=pl.ANY)
    vmem = pl.BlockSpec(memory_space=pltpu.VMEM)
    return pl.pallas_call(
        functools.partial(kernel, n, width * 4),
        out_shape=jax.ShapeDtypeStruct((T, width), bf16),
        in_specs=[anywhere, vmem, anywhere, anywhere, anywhere],
        out_specs=vmem,
        scratch_shapes=[
            pltpu.VMEM((4, 2, width, F), bf16),
            pltpu.VMEM((4, F, width), bf16),
            pltpu.VMEM((n, T, width), bf16),
            pltpu.VMEM((n, 2, 2, T, F), bf16),
            pltpu.VMEM((n, 2, 2, T, F), bf16),
            pltpu.VMEM((n, 2, T, F), bf16),
            pltpu.VMEM((n, 2, T, F), bf16),
            pltpu.VMEM((2, 2, T, F), f32),
            pltpu.VMEM((2, T, F), f32),
            pltpu.VMEM((n, 4, T, F), bf16),
            pltpu.VMEM((n, 8, T), f32),
            pltpu.VMEM((n, 3, 8, T), f32),
            pltpu.VMEM((n, 2, T // 2, width), bf16),
            pltpu.VMEM((n, 2, T // 2, width), bf16),
            pltpu.VMEM((T, width), f32),
            dma((3, 4)), dma(()),
            dma((n,)), dma((n,)),
            dma((n, 2, 2)), dma((n, 2, 2)),
            dma((n, 2)), dma((n, 2)),
            dma((n, 3, 2)), dma((n, 3, 2)),
            dma((n, 3)), dma((n, 3)),
            dma((n, 2)), dma((n, 2)),
        ],
        compiler_params=pltpu.CompilerParams(
            collective_id=0, has_side_effects=True, vmem_limit_bytes=58 * 1024 * 1024
        ),
    )(tokens, norm_gain[None, :], gate_weight, up_weight, down_weight)


def solution(mesh):
    placed = (
        P(("groups", "row"), "col"),
        P("col"),
        P("col", "row"),
        P("col", "row"),
        P("row", "col"),
    )
    return jax.shard_map(
        functools.partial(per_device, mesh.shape["row"]),
        mesh=mesh,
        in_specs=placed,
        out_specs=P(("groups", "row"), "col"),
        check_vma=False,
    )
```

```python
import functools
import jax
import jax.numpy as jnp
from jax import lax
from jax.experimental import pallas as pl
from jax.experimental.pallas import tpu as pltpu
from jax.sharding import PartitionSpec as P

epsilon = 1e-05
MESH = pl.DeviceIdType.MESH
f32 = jnp.float32
bf16 = jnp.bfloat16


def remote(src, dst, send, recv, device):
    return pltpu.make_async_remote_copy(
        src_ref=src, dst_ref=dst, send_sem=send, recv_sem=recv, device_id=device, device_id_type=MESH
    )


def kernel(n, width_total, tok, gain, gate_w, up_w, down_w, out,
           w_v, wd_v, xg, a_s, a_r, b_s, b_r, p_own, p_b, hid, q_s, q_r, o_s, o_r, total, xs,
           w_sem, own_sem, t_ss, t_rs, a_ss, a_rs, b_ss, b_rs, h_ss, h_rs, q_ss, q_rs, o_ss, o_rs):
    T, width = tok.shape
    rows = T // 2
    F = gate_w.shape[1] // 4
    tile_f = min(512, F)
    tile_d = min(512, width)
    row = lax.axis_index("row")
    col = lax.axis_index("col")
    hi, lo = col // 2, col % 2
    sibling = hi * 2 + (1 - lo)
    across = (1 - hi) * 2 + lo
    diagonal = (1 - hi) * 2 + (1 - lo)
    shards = (diagonal, across, sibling, col)

    def shift(step):
        late = jnp.where(step == n - 1, n - 1, jnp.where(step == n - 2, 1, step + 1))
        return jnp.where(step == 0, 0, late)

    def row_at(step):
        return lax.rem(row + shift(step), n)

    def row_back(step):
        return lax.rem(row + n - shift(step), n)

    def load(role, g):
        at = pl.ds(pl.multiple_of(shards[role] * F, F), F)
        source = (gate_w, up_w)[g].at[:, at]
        return pltpu.make_async_copy(source, w_v.at[role, g], w_sem.at[g, role])

    def load_down(role):
        at = pl.ds(pl.multiple_of(shards[role] * F, F), F)
        return pltpu.make_async_copy(down_w.at[at, :], wd_v.at[role], w_sem.at[2, role])

    def send_tokens(i):
        return remote(tok, xg.at[i], t_ss.at[i], t_rs.at[i], {"row": row_back(i)})

    def send_half(i, which, g):
        return remote(a_s.at[i, which, g], a_r.at[i, which, g],
                      a_ss.at[i, which, g], a_rs.at[i, which, g], {"col": sibling})

    def send_chip(i, g):
        return remote(b_s.at[i, g], b_r.at[i, g], b_ss.at[i, g], b_rs.at[i, g], {"col": across})

    def send_hidden(i, which, half):
        source, target, device = ((3, 1, across), (3, 2, sibling), (1, 0, sibling))[which]
        at = pl.ds(half * rows, rows)
        return remote(hid.at[i, source, at], hid.at[i, target, at],
                      h_ss.at[i, which, half], h_rs.at[i, which, half], {"col": device})

    def send_squares(i, role):
        return remote(q_s.at[i], q_r.at[i, role], q_ss.at[i, role], q_rs.at[i, role], {"col": shards[role]})

    def send_out(i, half):
        return remote(o_s.at[i, half], o_r.at[i, half], o_ss.at[i, half], o_rs.at[i, half], {"row": row_at(i)})

    own_tokens = pltpu.make_async_copy(tok, xg.at[0], own_sem)
    own_tokens.start()
    for g in range(2):
        for role in range(2):
            load(role, g).start()

    barrier = pltpu.get_barrier_semaphore()

    @pl.loop(1, n)
    def _(i):
        pl.semaphore_signal(barrier, inc=1, device_id={"row": row_at(i)}, device_id_type=MESH)

    for peer in shards[:3]:
        pl.semaphore_signal(barrier, inc=1, device_id={"col": peer}, device_id_type=MESH)
    pl.semaphore_wait(barrier, n + 2)

    if n > 1:
        send_tokens(1).start()

    for role in range(2, 4):
        for g in range(2):
            load(role, g).start()
    for role in range(4):
        load_down(role).start()

    def project(i, role, g, store):
        @pl.when(i == 0)
        def _():
            load(role, g).wait()

        x = xs[...]

        @pl.loop(0, F // tile_f)
        def _(t):
            at = pl.ds(pl.multiple_of(t * tile_f, tile_f), tile_f)
            store(g, at, jnp.dot(x, w_v[role, g, :, at], preferred_element_type=f32))

    def squares_of(i):
        x = xg[i].astype(f32)
        squares = x * x
        lanes = squares[:, :128]
        for c in range(1, width // 128):
            lanes = lanes + squares[:, c * 128:(c + 1) * 128]
        q_s[i] = jnp.broadcast_to(jnp.sum(lanes.T, axis=0, keepdims=True), (8, T))
        for role in range(3):
            send_squares(i, role).start()

    def partials(i):
        @pl.when(i == 0)
        def _():
            own_tokens.wait()

        @pl.when(i > 0)
        def _():
            send_tokens(i).wait_recv()

        @pl.when((i > 0) & (i + 1 < n))
        def _():
            send_tokens(i + 1).start()

        xs[...] = (xg[i].astype(f32) * gain[...]).astype(bf16)

        def to_half(which):
            def store(g, at, value):
                a_s[i, which, g, :, at] = value.astype(bf16)
            return store

        def to_chip(g, at, value):
            p_b[g, :, at] = value

        def to_own(g, at, value):
            p_own[lax.rem(i, 2), g, :, at] = value

        for g in range(2):
            project(i, 0, g, to_half(0))
            send_half(i, 0, g).start()
            project(i, 1, g, to_chip)
            send_half(i, 0, g).wait_recv()

            @pl.loop(0, F // tile_f)
            def _(t):
                at = pl.ds(pl.multiple_of(t * tile_f, tile_f), tile_f)
                b_s[i, g, :, at] = (p_b[g, :, at] + a_r[i, 0, g, :, at].astype(f32)).astype(bf16)

            send_chip(i, g).start()

        squares_of(i)
        for g in range(2):
            project(i, 2, g, to_half(1))
            send_half(i, 1, g).start()
        for g in range(2):
            project(i, 3, g, to_own)

    def activate(i):
        for role in range(3):
            send_squares(i, role).wait_recv()
        for g in range(2):
            send_half(i, 1, g).wait_recv()
            send_chip(i, g).wait_recv()
        all_squares = q_s[i] + q_r[i, 0] + q_r[i, 1] + q_r[i, 2]
        inverse = lax.rsqrt(all_squares / width_total + epsilon)
        inverse = jnp.broadcast_to(inverse[0:1, :], (128, T)).T[:, 0:1]
        slot = lax.rem(i, 2)

        for half in range(2):
            part = pl.ds(half * rows, rows)
            factor = inverse[half * rows:(half + 1) * rows]

            @pl.loop(0, F // tile_f)
            def _(t):
                at = pl.ds(pl.multiple_of(t * tile_f, tile_f), tile_f)
                gate, up = (
                    (p_own[slot, g, part, at] + a_r[i, 1, g, part, at].astype(f32)
                     + b_r[i, g, part, at].astype(f32)) * factor
                    for g in range(2)
                )
                hid[i, 3, part, at] = (gate / (1.0 + jnp.exp(-gate)) * up).astype(bf16)

            send_hidden(i, 0, half).start()
            send_hidden(i, 1, half).start()

    def lower(i):
        @pl.when(i == 0)
        def _():
            for role in range(4):
                load_down(role).wait()

        for half in range(2):
            send_hidden(i, 1, half).wait_recv()

        def product(role, part, at):
            return jnp.dot(hid[i, role, part], wd_v[role, :, at], preferred_element_type=f32)

        @pl.loop(0, width // tile_d)
        def _(t):
            at = pl.ds(pl.multiple_of(t * tile_d, tile_d), tile_d)
            every = pl.ds(0, T)
            total[:, at] = product(3, every, at) + product(2, every, at)

        for half in range(2):
            part = pl.ds(half * rows, rows)
            send_hidden(i, 0, half).wait_recv()
            send_hidden(i, 2, half).start()

            @pl.loop(0, width // tile_d)
            def _(t):
                at = pl.ds(pl.multiple_of(t * tile_d, tile_d), tile_d)
                total[part, at] += product(1, part, at)

            send_hidden(i, 2, half).wait_recv()

            @pl.loop(0, width // tile_d)
            def _(t):
                at = pl.ds(pl.multiple_of(t * tile_d, tile_d), tile_d)
                o_s[i, half, :, at] = (total[part, at] + product(0, part, at)).astype(bf16)

            @pl.when(i > 0)
            def _():
                send_out(i, half).start()

    @pl.loop(0, n + 2)
    def _(step):
        @pl.when(step < n)
        def _():
            partials(step)

        @pl.when((step >= 1) & (step < n + 1))
        def _():
            activate(step - 1)

        @pl.when(step >= 2)
        def _():
            lower(step - 2)

    for half in range(2):
        @pl.loop(1, n)
        def _(i):
            send_out(i, half).wait_recv()

        @pl.loop(0, width // tile_d)
        def _(t):
            at = pl.ds(pl.multiple_of(t * tile_d, tile_d), tile_d)
            out[pl.ds(half * rows, rows), at] = lax.fori_loop(
                1, n, lambda i, so_far: so_far + o_r[i, half, :, at].astype(f32), o_s[0, half, :, at].astype(f32)
            ).astype(bf16)

    @pl.loop(0, n)
    def _(i):
        @pl.when(i > 0)
        def _():
            send_tokens(i).wait_send()
            send_out(i, 0).wait_send()
            send_out(i, 1).wait_send()

        for piece in range(2):
            send_half(i, 0, piece).wait_send()
            send_half(i, 1, piece).wait_send()
            send_chip(i, piece).wait_send()
        for which in range(3):
            for half in range(2):
                send_hidden(i, which, half).wait_send()
            send_squares(i, which).wait_send()


def per_device(n, tokens, norm_gain, gate_weight, up_weight, down_weight):
    T, width = tokens.shape
    F = gate_weight.shape[1] // 4
    dma = pltpu.SemaphoreType.DMA
    anywhere = pl.BlockSpec(memory_space=pl.ANY)
    vmem = pl.BlockSpec(memory_space=pltpu.VMEM)
    return pl.pallas_call(
        functools.partial(kernel, n, width * 4),
        out_shape=jax.ShapeDtypeStruct((T, width), bf16),
        in_specs=[anywhere, vmem, anywhere, anywhere, anywhere],
        out_specs=vmem,
        scratch_shapes=[
            pltpu.VMEM((4, 2, width, F), bf16),
            pltpu.VMEM((4, F, width), bf16),
            pltpu.VMEM((n, T, width), bf16),
            pltpu.VMEM((n, 2, 2, T, F), bf16),
            pltpu.VMEM((n, 2, 2, T, F), bf16),
            pltpu.VMEM((n, 2, T, F), bf16),
            pltpu.VMEM((n, 2, T, F), bf16),
            pltpu.VMEM((2, 2, T, F), f32),
            pltpu.VMEM((2, T, F), f32),
            pltpu.VMEM((n, 4, T, F), bf16),
            pltpu.VMEM((n, 8, T), f32),
            pltpu.VMEM((n, 3, 8, T), f32),
            pltpu.VMEM((n, 2, T // 2, width), bf16),
            pltpu.VMEM((n, 2, T // 2, width), bf16),
            pltpu.VMEM((T, width), f32),
            pltpu.VMEM((T, width), bf16),
            dma((3, 4)), dma(()),
            dma((n,)), dma((n,)),
            dma((n, 2, 2)), dma((n, 2, 2)),
            dma((n, 2)), dma((n, 2)),
            dma((n, 3, 2)), dma((n, 3, 2)),
            dma((n, 3)), dma((n, 3)),
            dma((n, 2)), dma((n, 2)),
        ],
        compiler_params=pltpu.CompilerParams(
            collective_id=0, has_side_effects=True, vmem_limit_bytes=58 * 1024 * 1024
        ),
    )(tokens, norm_gain[None, :], gate_weight, up_weight, down_weight)


def solution(mesh):
    placed = (
        P(("groups", "row"), "col"),
        P("col"),
        P("col", "row"),
        P("col", "row"),
        P("row", "col"),
    )
    return jax.shard_map(
        functools.partial(per_device, mesh.shape["row"]),
        mesh=mesh,
        in_specs=placed,
        out_specs=P(("groups", "row"), "col"),
        check_vma=False,
    )
```
